256 devices in a mesh: fsdp: 8 (over y, core), tp: 16 (over x_lo, z), layer: 2 (over x_hi).
Axes of the slice: x: 4 (x_hi: 2, x_lo: 2; x = x_hi * 2 + x_lo), y: 4, z: 8, core: 2. Of those that a mesh axis runs over, the one named last changes fastest.
Arguments:
- gradient: bfloat16 [8192, 14336], P('fsdp', ('tp', 'layer')), may hold values from -6 to 6
- left_basis: bfloat16 [8192, 8192], P('fsdp', ('tp', 'layer')), may hold values from -0.0625 to 0.0625
- first_moment: float32 [8192, 14336], P('fsdp', ('tp', 'layer')), may hold values from -4 to 4
- second_moment: float32 [8192, 14336], P('fsdp', ('tp', 'layer')), may hold values from 0.05 to 5
Outputs:
- update: bfloat16 [8192, 14336], P('fsdp', ('tp', 'layer'))
- first_new: float32 [8192, 14336], P('fsdp', ('tp', 'layer'))
- second_new: float32 [8192, 14336], P('fsdp', ('tp', 'layer'))
The draws below stay inside these ranges and needn't reach their ends.
All inputs are finite; a program needn't handle non-finite values.
Results may differ from the reference program's by a relative error of at most 0.012.
Values may be sent and summed in bfloat16 or wider, within the bound.
A program may use at most 128 MiB of HBM per device.

```python
import math
import jax
import jax.numpy as jnp
from jax import lax

D = 8192
F = 14336
STEP = 20
N_FSDP = 8


def block_levels(rng, shape, shards, least, top_value):
    level = 1.0
    for dim, blocks in shards:
        draws = jax.random.uniform(jax.random.fold_in(jax.random.fold_in(rng, 6), dim), (blocks,), jnp.float32, least / len(shards), top_value / len(shards))
        level = level * jnp.repeat(jnp.exp(draws), shape[dim] // blocks).reshape((-1,) + (1,) * (len(shape) - 1 - dim))
    return level


def normal_values(key, extent, deviation, bound, shards=(), kind=jnp.bfloat16):
    array = deviation * jax.random.normal(key, extent, jnp.float32)
    if shards:
        array = array * block_levels(key, extent, shards, -0.22, 0.18)
    return jnp.clip(array, -bound, bound).astype(kind)


def setup_inputs(seed: int = 0) -> dict:
    key_list = jax.random.split(jax.random.key(seed), 5)
    return {
        "gradient": normal_values(key_list[0], (D, F), 1.0, 6.0, ((0, 8), (1, 32))),
        "left_basis": normal_values(key_list[1], (D, D), D ** -0.5, 0.0625, ((0, 8), (1, 32))),
        "first_moment": normal_values(key_list[2], (D, F), 0.5, 4.0, ((0, 8), (1, 32)), jnp.float32),
        "second_moment": jnp.clip(jnp.exp(math.log(5.0) - 4.6051702 * jax.random.uniform(key_list[3], (D, F), jnp.float32) ** block_levels(key_list[3], (D, F), ((0, 8), (1, 32)), -0.2, 0.2)), 0.05, 5.0),
    }


beta_one = 0.9
beta_two = 0.95
adam_epsilon = 1e-08

def reference(gradient, left_basis, first_moment, second_moment):
    row_count = D // N_FSDP

    def add_block(running, position):
        grad_rows = lax.dynamic_slice_in_dim(gradient, position * row_count, row_count, 0)
        basis_rows = lax.dynamic_slice_in_dim(left_basis, position * row_count, row_count, 0)
        partial_sum = lax.dot_general(basis_rows, grad_rows, (((0,), (0,)), ((), ())), preferred_element_type=jnp.float32)
        rounded = lax.optimization_barrier(partial_sum.astype(jnp.bfloat16))
        return (running + rounded.astype(jnp.float32), None)
    rotated, _ = lax.scan(add_block, jnp.zeros((D, F), jnp.float32), jnp.arange(N_FSDP, dtype=jnp.int32))
    first_new = beta_one * first_moment + (1.0 - beta_one) * rotated
    second_new = beta_two * second_moment + (1.0 - beta_two) * rotated * rotated
    correct_one = 1.0 - beta_one ** STEP
    correct_two = 1.0 - beta_two ** STEP
    direction = (first_new / correct_one / (jnp.sqrt(second_new / correct_two) + adam_epsilon)).astype(jnp.bfloat16)
    update = jnp.dot(left_basis, direction, preferred_element_type=jnp.float32).astype(jnp.bfloat16)
    return (update, first_new, second_new)
```

```python
import jax
import jax.numpy as jnp
from jax import lax
from jax.experimental import pallas as pl
from jax.experimental.pallas import tpu as pltpu
from jax.sharding import PartitionSpec as P

STEP = 20


beta_one = 0.9
beta_two = 0.95
adam_epsilon = 1e-08
correct_one = 1.0 - beta_one**STEP
correct_two = 1.0 - beta_two**STEP

MESH = pl.DeviceIdType.MESH
BF16 = jnp.bfloat16
F32 = jnp.float32

ROWS, COLS, WIDE = 1024, 448, 256
HALF = COLS // 2
NX, NY, NZ = 4, 4, 8
CHUNKS = NX * NZ

PART_P = 608
SPANS = {
    ("P", "F"): (0, PART_P),
    ("P", "A"): (0, PART_P // 2),
    ("P", "B"): (PART_P // 2, PART_P // 2),
    ("Q", "F"): (PART_P, ROWS - PART_P),
    ("Q", "A"): (PART_P, (ROWS - PART_P) // 2),
    ("Q", "B"): ((PART_P + ROWS) // 2, (ROWS - PART_P) // 2),
}
ORDER = (
    (0, 0), (-1, 0), (1, 0), (0, -1), (0, 1), (-1, -1), (1, -1), (-1, 1), (1, 1), (2, 0), (0, -2), (0, 2), (2, -1), (2, 1), (-1, -2), (1, -2), (-1, 2), (1, 2), (0, -3), (0, 3), (2, -2), (2, 2), (-1, -3), (1, -3), (-1, 3), (1, 3), (0, 4), (2, -3), (2, 3), (-1, 4), (1, 4), (2, 4),
)
ARRIVALS = (
    (),
    (("Q", -1, 0, "F"), ("Q", 1, 0, "F"), ("P", 0, -1, "F"), ("P", 0, 1, "F"), ("P", -1, 0, "F"), ("P", 1, 0, "F"), ("Q", 0, -1, "F"), ("Q", 0, 1, "F"),),
    (),
    (("Q", 2, 0, "A"), ("Q", 2, 0, "B"),),
    (("Q", -1, -1, "F"), ("Q", -1, 1, "F"),),
    (("P", -1, -1, "F"), ("P", 1, -1, "F"), ("Q", 1, -1, "F"), ("Q", 1, 1, "F"),),
    (),
    (("P", -1, 1, "F"), ("P", 1, 1, "F"), ("P", 0, -2, "F"), ("P", 0, 2, "F"),),
    (),
    (("P", 2, 0, "A"), ("P", 2, 0, "B"),),
    (("Q", 0, -2, "F"), ("Q", 0, 2, "F"),),
    (),
    (("P", 2, -1, "A"), ("P", 2, -1, "B"), ("Q", 2, -1, "A"), ("Q", 2, 1, "A"), ("Q", 2, -1, "B"), ("Q", 2, 1, "B"),),
    (("P", 2, 1, "A"), ("P", 2, 1, "B"),),
    (("Q", -1, -2, "F"), ("Q", -1, 2, "F"), ("P", -1, -2, "F"), ("P", 1, -2, "F"),),
    (("Q", 1, -2, "F"), ("Q", 1, 2, "F"),),
    (("P", -1, 2, "F"), ("P", 1, 2, "F"),),
    (),
    (("P", 0, -3, "F"), ("P", 0, 3, "F"), ("P", 2, -2, "A"), ("P", 2, -2, "B"), ("Q", 0, -3, "F"), ("Q", 0, 3, "F"),),
    (("P", 2, 2, "A"), ("P", 2, 2, "B"),),
    (("Q", 2, -2, "A"), ("Q", 2, 2, "A"), ("Q", 2, -2, "B"), ("Q", 2, 2, "B"),),
    (),
    (("P", -1, -3, "F"), ("P", 1, -3, "F"), ("Q", -1, -3, "F"), ("Q", -1, 3, "F"),),
    (("Q", 1, -3, "F"), ("Q", 1, 3, "F"), ("P", -1, 3, "F"), ("P", 1, 3, "F"),),
    (),
    (),
    (("P", 0, 4, "A"), ("P", 0, 4, "B"), ("P", 2, -3, "A"), ("P", 2, -3, "B"), ("Q", 0, 4, "A"), ("Q", 0, 4, "B"),),
    (("P", 2, 3, "A"), ("P", 2, 3, "B"), ("Q", 2, -3, "A"), ("Q", 2, 3, "A"), ("P", -1, 4, "A"), ("P", 1, 4, "A"), ("Q", 2, -3, "B"), ("Q", 2, 3, "B"),),
    (),
    (("Q", -1, 4, "A"), ("Q", -1, 4, "B"), ("P", -1, 4, "B"), ("P", 1, 4, "B"),),
    (("Q", 1, 4, "A"), ("Q", 1, 4, "B"),),
    (("P", 2, 4, "A"), ("Q", 2, 4, "A"), ("Q", 2, 4, "B"), ("P", 2, 4, "B"),),
)
SLOT = {offset: slot for slot, offset in enumerate(ORDER)}

LAG_SUM, LAG_OWN, LAG_PASS, LAG_UPDATE = 1, 5, 8, 10


def bits(values, shift):
    word = sum((((value >> shift) & 1) << k) for k, value in enumerate(values))
    return word - (1 << 32) if word >= 1 << 31 else word


X_BITS = [bits([i % NX for i, _ in ORDER], s) for s in range(2)]
Z_BITS = [bits([j % NZ for _, j in ORDER], s) for s in range(3)]


def lookup(words, t):
    total = 0
    for s, word in enumerate(words):
        total = total + (lax.shift_right_logical(jnp.int32(word), t) & 1) * (1 << s)
    return total


def onward(part, i, j, half):
    out = []
    if part == "P":
        if i == 0:
            if j == 0:
                out += [("z+", "F"), ("z-", "F")]
            elif j in (-1, -2):
                out += [("z+", "F")]
            elif j in (1, 2):
                out += [("z-", "F")]
            elif j == -3:
                out += [("z+", "A")]
            elif j == 3:
                out += [("z-", "B")]
            out += [("x+", half), ("x-", half)]
        elif i == -1 and half in "FA":
            out += [("x+", "A")]
        elif i == 1 and half in "FB":
            out += [("x-", "B")]
    elif j == 0:
        if i == 0:
            out += [("x+", "F"), ("x-", "F")]
        elif i == -1:
            out += [("x+", "A")]
        elif i == 1:
            out += [("x-", "B")]
        out += [("z+", half), ("z-", half)]
    elif j in (-1, -2):
        out += [("z+", half)]
    elif j in (1, 2):
        out += [("z-", half)]
    elif j == -3 and half in "FA":
        out += [("z+", "A")]
    elif j == 3 and half in "FB":
        out += [("z-", "B")]
    return out


def seen_from(link, i, j):
    i += {"x+": -1, "x-": 1}.get(link, 0)
    j += {"z+": -1, "z-": 1}.get(link, 0)
    return (i + 1) % NX - 1, (j + 3) % NZ - 3


def kernel(
    grad_hbm, basis_hbm, first_hbm, second_hbm,
    update_hbm, first_out, second_out,
    panel, grad, grad_t, first, second, own, pair_out, pair_in, sum_out, sum_in, turned, steps, total, update,
    load_sem, store_sem, chunk_sem, chunk_sent, pair_sem, pair_sent, sum_sem, sum_sent, near_sem, far_sem, step_sent,
):
    f, tp, layer = lax.axis_index("fsdp"), lax.axis_index("tp"), lax.axis_index("layer")
    x, y, z, c = layer * 2 + tp // NZ, f // 2, tp % NZ, f % 2

    def place(px, py, pz, pc):
        return (py * 2 + pc, (px % 2) * NZ + pz, px // 2)

    partner = place(x, y, z, 1 - c)
    neighbours = {
        "x+": place((x + 1) % NX, y, z, c),
        "x-": place((x + NX - 1) % NX, y, z, c),
        "z+": place(x, y, (z + 1) % NZ, c),
        "z-": place(x, y, (z + NZ - 1) % NZ, c),
    }

    def remote(source, target, send_sem, recv_sem, device):
        return pltpu.make_async_remote_copy(
            src_ref=source, dst_ref=target, send_sem=send_sem, recv_sem=recv_sem, device_id=device, device_id_type=MESH
        )

    def await_bytes(ref, sem):
        pltpu.make_async_copy(ref, ref, sem).wait()

    loads = [
        pltpu.make_async_copy(basis_hbm, panel.at[0], load_sem.at[0]),
        pltpu.make_async_copy(grad_hbm, grad, load_sem.at[1]),
        pltpu.make_async_copy(first_hbm, first, load_sem.at[2]),
        pltpu.make_async_copy(second_hbm, second, load_sem.at[3]),
    ]
    for load in loads:
        load.start()

    barrier = pltpu.get_barrier_semaphore()
    peers = list(neighbours.values()) + [partner]
    for k in range(1, NY):
        for pc in range(2):
            peers.append(place(x, (y + k) % NY, z, pc))
    for peer in peers:
        pl.semaphore_signal(barrier, inc=1, device_id=peer, device_id_type=MESH)
    loads[0].wait()
    pl.semaphore_wait(barrier, len(peers))

    def chunk_piece(part, half, slot):
        start, size = SPANS[part, half]
        return panel.at[slot, pl.ds(start, size)], chunk_sem.at[slot, 2 * (part == "Q") + (half == "B")]

    def hand_on(part, i, j, link, half):
        start, size = SPANS[part, half]
        target, sem = chunk_piece(part, half, SLOT[seen_from(link, i, j)])
        remote(panel.at[SLOT[i, j], pl.ds(start, size)], target, chunk_sent, sem, neighbours[link]).start()

    for link in ("x+", "x-"):
        hand_on("Q", 0, 0, link, "F")
    for link in ("z+", "z-"):
        hand_on("P", 0, 0, link, "F")
    for link in ("x+", "x-"):
        hand_on("P", 0, 0, link, "F")
    for link in ("z+", "z-"):
        hand_on("Q", 0, 0, link, "F")

    loads[1].wait()
    for k in range(ROWS // 256):
        block = jnp.concatenate(
            [grad[pl.ds(256 * k, 256), :].astype(F32), jnp.zeros((256, 512 - COLS), F32)], axis=1
        ).T.astype(BF16)
        for h in range(2):
            at = pl.multiple_of(jnp.where(c == h, HALF, 0), 16)
            grad_t[pl.ds(at, HALF), pl.ds(256 * k, 256)] = block[HALF * h : HALF * (h + 1)]
    total[...] = jnp.zeros_like(total)
    turned[pl.ds(COLS, 512 - COLS), :] = jnp.zeros((512 - COLS, WIDE), F32)
    loads[2].wait()
    loads[3].wait()

    def owner_of(t):
        xs, zs = lax.rem(x + lookup(X_BITS, t), NX), lax.rem(z + lookup(Z_BITS, t), NZ)
        return 2 * lax.rem(xs, 2) + zs // 4, lax.rem(zs // 2, 2), 2 * lax.rem(zs, 2) + xs // 2

    def first_product(t):
        product = jnp.dot(grad_t[...], panel[t], preferred_element_type=F32)
        pair_out[t] = product[:HALF].astype(BF16)
        remote(pair_out.at[t], pair_in.at[t], pair_sent, pair_sem.at[t], partner).start()
        own[lax.rem(t, 2)] = product[HALF:]

    def chip_sum(t):
        await_bytes(pair_in.at[t], pair_sem.at[t])
        oy, oc, block = owner_of(t)
        mine = (own[lax.rem(t, 2)] + pair_in[t].astype(F32)).astype(BF16)
        here = (oy == y) & (oc == c)

        @pl.when(here)
        def _():
            sum_in[block, 0] = mine

        @pl.when(jnp.logical_not(here))
        def _():
            sum_out[t] = mine
            place_in = 2 * lax.rem(y - oy + NY, NY) + jnp.where(oc == c, 0, 1)
            remote(
                sum_out.at[t], sum_in.at[block, place_in], sum_sent, sum_sem.at[block, place_in], place(x, oy, z, oc)
            ).start()

    def own_step(t):
        oy, oc, block = owner_of(t)

        @pl.when((oy == y) & (oc == c))
        def _():
            for r in range(1, 2 * NY):
                await_bytes(sum_in.at[block, r], sum_sem.at[block, r])
            for e in range(2):
                rotated = sum_in[block, e].astype(F32)
                for k in range(1, NY):
                    rotated = rotated + sum_in[block, 2 * k + e].astype(F32)
                at = pl.multiple_of(HALF * (c if e == 0 else 1 - c), 8)
                turned[pl.ds(at, HALF), :] = rotated
            for k in range(WIDE // 128):
                rows = pl.ds(pl.multiple_of(block * WIDE + 128 * k, 128), 128)
                rotated = turned[:, pl.ds(128 * k, 128)].T[:, :COLS]
                first_new = beta_one * first[rows, :] + (1.0 - beta_one) * rotated
                second_new = beta_two * second[rows, :] + (1.0 - beta_two) * rotated * rotated
                step = first_new / correct_one / (jnp.sqrt(second_new / correct_two) + adam_epsilon)
                first[rows, :] = first_new
                second[rows, :] = second_new
                step = jnp.concatenate([step, jnp.zeros((128, 512 - COLS), F32)], axis=1).T
                steps[t, :, pl.ds(128 * k, 128)] = step[:COLS].astype(BF16)
            for h in range(2):
                half = pl.ds(HALF * h, HALF)
                for k in range(1, NY):
                    remote(
                        steps.at[t, half], steps.at[t, half], step_sent, near_sem.at[t], place(x, lax.rem(y + k, NY), z, h)
                    ).start()
            remote(steps.at[t], steps.at[t], step_sent, near_sem.at[t], partner).start()
            rows = pl.ds(pl.multiple_of(block * WIDE, WIDE), WIDE)
            pltpu.make_async_copy(first.at[rows], first_out.at[rows], store_sem.at[0]).start()
            pltpu.make_async_copy(second.at[rows], second_out.at[rows], store_sem.at[1]).start()

    def pass_step(t):
        oy, _, _ = owner_of(t)

        @pl.when(oy != y)
        def _():
            half = steps.at[t, pl.ds(pl.multiple_of(HALF * c, 16), HALF)]
            await_bytes(half, near_sem.at[t])
            remote(half, half, step_sent, far_sem.at[t], partner).start()

    def second_product(t):
        oy, oc, _ = owner_of(t)

        @pl.when(oy != y)
        def _():
            await_bytes(steps.at[t, pl.ds(0, HALF)], far_sem.at[t])

        @pl.when((oy == y) & (oc != c))
        def _():
            await_bytes(steps.at[t], near_sem.at[t])

        for k in range(ROWS // 256):
            rows = pl.ds(256 * k, 256)
            total[rows, :] += lax.dot_general(
                panel[t, rows], steps[t], (((1,), (1,)), ((), ())), preferred_element_type=F32
            )

    def body(t, carry):
        for group in range(0, CHUNKS, 8):

            @pl.when((t >= group) & (t < group + 8))
            def _():
                for slot in range(group, group + 8):
                    if ARRIVALS[slot]:

                        @pl.when(t == slot)
                        def _():
                            for part, i, j, half in ARRIVALS[slot]:
                                await_bytes(*chunk_piece(part, half, SLOT[i, j]))
                                for link, piece in onward(part, i, j, half):
                                    hand_on(part, i, j, link, piece)

        def stage(lag, work):
            @pl.when((t >= lag) & (t < CHUNKS + lag))
            def _():
                work(t - lag)

        stage(LAG_SUM, chip_sum)
        stage(0, first_product)
        stage(LAG_OWN, own_step)
        stage(LAG_PASS, pass_step)
        stage(LAG_UPDATE, second_product)
        return carry

    lax.fori_loop(0, CHUNKS + LAG_UPDATE, body, 0)

    stores = []
    for k in range(4):
        rows = pl.ds(256 * k, 256)
        update[rows, :] = total[rows, :].astype(BF16)
        stores.append(pltpu.make_async_copy(update.at[rows], update_hbm.at[rows], store_sem.at[2]))
        stores[-1].start()
    await_bytes(panel.at[pl.ds(1, CHUNKS - 1)], chunk_sent)
    await_bytes(pair_out, pair_sent)
    await_bytes(sum_out.at[pl.ds(0, CHUNKS - 4)], sum_sent)
    await_bytes(steps.at[pl.ds(0, CHUNKS - 4)], step_sent)
    await_bytes(first, store_sem.at[0])
    await_bytes(second, store_sem.at[1])
    await_bytes(update, store_sem.at[2])


def on_device(gradient, left_basis, first_moment, second_moment):
    dma = pltpu.SemaphoreType.DMA
    return pl.pallas_call(
        kernel,
        out_shape=(
            jax.ShapeDtypeStruct((ROWS, COLS), BF16),
            jax.ShapeDtypeStruct((ROWS, COLS), F32),
            jax.ShapeDtypeStruct((ROWS, COLS), F32),
        ),
        in_specs=[pl.BlockSpec(memory_space=pl.ANY)] * 4,
        out_specs=tuple([pl.BlockSpec(memory_space=pl.ANY)] * 3),
        scratch_shapes=[
            pltpu.VMEM((CHUNKS, ROWS, WIDE), BF16),
            pltpu.VMEM((ROWS, COLS), BF16),
            pltpu.VMEM((COLS, ROWS), BF16),
            pltpu.VMEM((ROWS, COLS), F32),
            pltpu.VMEM((ROWS, COLS), F32),
            pltpu.VMEM((2, HALF, WIDE), F32),
            pltpu.VMEM((CHUNKS, HALF, WIDE), BF16),
            pltpu.VMEM((CHUNKS, HALF, WIDE), BF16),
            pltpu.VMEM((CHUNKS, HALF, WIDE), BF16),
            pltpu.VMEM((4, 2 * NY, HALF, WIDE), BF16),
            pltpu.VMEM((512, WIDE), F32),
            pltpu.VMEM((CHUNKS, COLS, WIDE), BF16),
            pltpu.VMEM((ROWS, COLS), F32),
            pltpu.VMEM((ROWS, COLS), BF16),
            dma((4,)),
            dma((3,)),
            dma((CHUNKS, 4)),
            dma,
            dma((CHUNKS,)),
            dma,
            dma((4, 2 * NY)),
            dma,
            dma((CHUNKS,)),
            dma((CHUNKS,)),
            dma,
        ],
        compiler_params=pltpu.CompilerParams(
            collective_id=0, has_side_effects=True, vmem_limit_bytes=60 << 20
        ),
        cost_estimate=pl.CostEstimate(flops=4 * 8192 * ROWS * COLS, bytes_accessed=10 << 20, transcendentals=0),
    )(gradient, left_basis, first_moment, second_moment)


def solution(mesh):
    placed = P("fsdp", ("tp", "layer"))
    return jax.shard_map(
        on_device, mesh=mesh, in_specs=(placed,) * 4, out_specs=(placed,) * 3, check_vma=False
    )
```

```python
import jax
import jax.numpy as jnp
from jax import lax
from jax.experimental import pallas as pl
from jax.experimental.pallas import tpu as pltpu
from jax.sharding import PartitionSpec as P

STEP = 20


beta_one = 0.9
beta_two = 0.95
adam_epsilon = 1e-08
correct_one = 1.0 - beta_one**STEP
correct_two = 1.0 - beta_two**STEP

MESH = pl.DeviceIdType.MESH
BF16 = jnp.bfloat16
F32 = jnp.float32

ROWS, COLS, WIDE = 1024, 448, 256
HALF = COLS // 2
QUARTER = HALF // 2
NX, NY, NZ = 4, 4, 8
CHUNKS = NX * NZ

PART_P = 608
SPANS = {
    ("P", "F"): (0, PART_P),
    ("P", "A"): (0, PART_P // 2),
    ("P", "B"): (PART_P // 2, PART_P // 2),
    ("Q", "F"): (PART_P, ROWS - PART_P),
    ("Q", "A"): (PART_P, (ROWS - PART_P) // 2),
    ("Q", "B"): ((PART_P + ROWS) // 2, (ROWS - PART_P) // 2),
}
ORDER = (
    (0, 0), (-1, 0), (1, 0), (0, -1), (0, 1), (-1, -1), (1, -1), (-1, 1), (1, 1), (2, 0), (0, -2), (0, 2), (2, -1), (2, 1), (-1, -2), (1, -2), (-1, 2), (1, 2), (0, -3), (0, 3), (2, -2), (2, 2), (-1, -3), (1, -3), (-1, 3), (1, 3), (0, 4), (2, -3), (2, 3), (-1, 4), (1, 4), (2, 4),
)
ARRIVALS = (
    (),
    (("Q", -1, 0, "F"), ("Q", 1, 0, "F"), ("P", 0, -1, "F"), ("P", 0, 1, "F"), ("P", -1, 0, "F"), ("P", 1, 0, "F"), ("Q", 0, -1, "F"), ("Q", 0, 1, "F"),),
    (),
    (("Q", 2, 0, "A"), ("Q", 2, 0, "B"),),
    (("Q", -1, -1, "F"), ("Q", -1, 1, "F"),),
    (("P", -1, -1, "F"), ("P", 1, -1, "F"), ("Q", 1, -1, "F"), ("Q", 1, 1, "F"),),
    (),
    (("P", -1, 1, "F"), ("P", 1, 1, "F"), ("P", 0, -2, "F"), ("P", 0, 2, "F"),),
    (),
    (("P", 2, 0, "A"), ("P", 2, 0, "B"),),
    (("Q", 0, -2, "F"), ("Q", 0, 2, "F"),),
    (),
    (("P", 2, -1, "A"), ("P", 2, -1, "B"), ("Q", 2, -1, "A"), ("Q", 2, 1, "A"), ("Q", 2, -1, "B"), ("Q", 2, 1, "B"),),
    (("P", 2, 1, "A"), ("P", 2, 1, "B"),),
    (("Q", -1, -2, "F"), ("Q", -1, 2, "F"), ("P", -1, -2, "F"), ("P", 1, -2, "F"),),
    (("Q", 1, -2, "F"), ("Q", 1, 2, "F"),),
    (("P", -1, 2, "F"), ("P", 1, 2, "F"),),
    (),
    (("P", 0, -3, "F"), ("P", 0, 3, "F"), ("P", 2, -2, "A"), ("P", 2, -2, "B"), ("Q", 0, -3, "F"), ("Q", 0, 3, "F"),),
    (("P", 2, 2, "A"), ("P", 2, 2, "B"),),
    (("Q", 2, -2, "A"), ("Q", 2, 2, "A"), ("Q", 2, -2, "B"), ("Q", 2, 2, "B"),),
    (),
    (("P", -1, -3, "F"), ("P", 1, -3, "F"), ("Q", -1, -3, "F"), ("Q", -1, 3, "F"),),
    (("Q", 1, -3, "F"), ("Q", 1, 3, "F"), ("P", -1, 3, "F"), ("P", 1, 3, "F"),),
    (),
    (),
    (("P", 0, 4, "A"), ("P", 0, 4, "B"), ("P", 2, -3, "A"), ("P", 2, -3, "B"), ("Q", 0, 4, "A"), ("Q", 0, 4, "B"),),
    (("P", 2, 3, "A"), ("P", 2, 3, "B"), ("Q", 2, -3, "A"), ("Q", 2, 3, "A"), ("P", -1, 4, "A"), ("P", 1, 4, "A"), ("Q", 2, -3, "B"), ("Q", 2, 3, "B"),),
    (),
    (("Q", -1, 4, "A"), ("Q", -1, 4, "B"), ("P", -1, 4, "B"), ("P", 1, 4, "B"),),
    (("Q", 1, 4, "A"), ("Q", 1, 4, "B"),),
    (("P", 2, 4, "A"), ("Q", 2, 4, "A"), ("Q", 2, 4, "B"), ("P", 2, 4, "B"),),
)
SLOT = {offset: slot for slot, offset in enumerate(ORDER)}

LAG_SUM, LAG_RELAY, LAG_OWN, LAG_PASS, LAG_FAR, LAG_UPDATE = 1, 4, 8, 11, 14, 16


def bits(values, shift):
    word = sum((((value >> shift) & 1) << k) for k, value in enumerate(values))
    return word - (1 << 32) if word >= 1 << 31 else word


X_BITS = [bits([i % NX for i, _ in ORDER], s) for s in range(2)]
Z_BITS = [bits([j % NZ for _, j in ORDER], s) for s in range(3)]


def lookup(words, t):
    total = 0
    for s, word in enumerate(words):
        total = total + (lax.shift_right_logical(jnp.int32(word), t) & 1) * (1 << s)
    return total


def onward(part, i, j, half):
    out = []
    if part == "P":
        if i == 0:
            if j == 0:
                out += [("z+", "F"), ("z-", "F")]
            elif j in (-1, -2):
                out += [("z+", "F")]
            elif j in (1, 2):
                out += [("z-", "F")]
            elif j == -3:
                out += [("z+", "A")]
            elif j == 3:
                out += [("z-", "B")]
            out += [("x+", half), ("x-", half)]
        elif i == -1 and half in "FA":
            out += [("x+", "A")]
        elif i == 1 and half in "FB":
            out += [("x-", "B")]
    elif j == 0:
        if i == 0:
            out += [("x+", "F"), ("x-", "F")]
        elif i == -1:
            out += [("x+", "A")]
        elif i == 1:
            out += [("x-", "B")]
        out += [("z+", half), ("z-", half)]
    elif j in (-1, -2):
        out += [("z+", half)]
    elif j in (1, 2):
        out += [("z-", half)]
    elif j == -3 and half in "FA":
        out += [("z+", "A")]
    elif j == 3 and half in "FB":
        out += [("z-", "B")]
    return out


def seen_from(link, i, j):
    i += {"x+": -1, "x-": 1}.get(link, 0)
    j += {"z+": -1, "z-": 1}.get(link, 0)
    return (i + 1) % NX - 1, (j + 3) % NZ - 3


def kernel(
    grad_hbm, basis_hbm, first_hbm, second_hbm,
    update_hbm, first_out, second_out,
    panel, grad, grad_t, first, second, own, pair_out, pair_in, sum_out, relay_in, sum_in, steps, total, update,
    load_sem, store_sem, chunk_sem, chunk_sent, pair_sem, pair_sent, relay_sem, sum_sem, sum_sent, near_sem, quarter_sem, other_sem, step_sent,
):
    f, tp, layer = lax.axis_index("fsdp"), lax.axis_index("tp"), lax.axis_index("layer")
    x, y, z, c = layer * 2 + tp // NZ, f // 2, tp % NZ, f % 2

    def place(px, py, pz, pc):
        return (py * 2 + pc, (px % 2) * NZ + pz, px // 2)

    partner = place(x, y, z, 1 - c)
    neighbours = {
        "x+": place((x + 1) % NX, y, z, c),
        "x-": place((x + NX - 1) % NX, y, z, c),
        "z+": place(x, y, (z + 1) % NZ, c),
        "z-": place(x, y, (z + NZ - 1) % NZ, c),
    }

    def remote(source, target, send_sem, recv_sem, device):
        return pltpu.make_async_remote_copy(
            src_ref=source, dst_ref=target, send_sem=send_sem, recv_sem=recv_sem, device_id=device, device_id_type=MESH
        )

    def await_bytes(ref, sem):
        pltpu.make_async_copy(ref, ref, sem).wait()

    loads = [
        pltpu.make_async_copy(basis_hbm, panel.at[0], load_sem.at[0]),
        pltpu.make_async_copy(grad_hbm, grad, load_sem.at[1]),
        pltpu.make_async_copy(first_hbm, first, load_sem.at[2]),
        pltpu.make_async_copy(second_hbm, second, load_sem.at[3]),
    ]
    for load in loads:
        load.start()

    barrier = pltpu.get_barrier_semaphore()
    peers = list(neighbours.values()) + [partner]
    for k in range(1, NY):
        for pc in range(2):
            peers.append(place(x, (y + k) % NY, z, pc))
    for peer in peers:
        pl.semaphore_signal(barrier, inc=1, device_id=peer, device_id_type=MESH)
    loads[0].wait()
    pl.semaphore_wait(barrier, len(peers))

    def chunk_piece(part, half, slot):
        start, size = SPANS[part, half]
        return panel.at[slot, pl.ds(start, size)], chunk_sem.at[slot, 2 * (part == "Q") + (half == "B")]

    def hand_on(part, i, j, link, half):
        start, size = SPANS[part, half]
        target, sem = chunk_piece(part, half, SLOT[seen_from(link, i, j)])
        remote(panel.at[SLOT[i, j], pl.ds(start, size)], target, chunk_sent, sem, neighbours[link]).start()

    for link in ("x+", "x-"):
        hand_on("Q", 0, 0, link, "F")
    for link in ("z+", "z-"):
        hand_on("P", 0, 0, link, "F")
    for link in ("x+", "x-"):
        hand_on("P", 0, 0, link, "F")
    for link in ("z+", "z-"):
        hand_on("Q", 0, 0, link, "F")

    loads[1].wait()
    for h in range(2):
        at = pl.multiple_of(jnp.where(c == h, HALF, 0), 16)
        grad_t[pl.ds(at, HALF), :] = grad[pl.ds(HALF * h, HALF), :]
    total[...] = jnp.zeros_like(total)
    loads[2].wait()
    loads[3].wait()

    def owner_of(t):
        xs, zs = lax.rem(x + lookup(X_BITS, t), NX), lax.rem(z + lookup(Z_BITS, t), NZ)
        return 2 * lax.rem(xs, 2) + zs // 4, lax.rem(zs // 2, 2), 2 * lax.rem(zs, 2) + xs // 2

    def first_product(t):
        product = jnp.dot(grad_t[...], panel[t], preferred_element_type=F32)
        pair_out[t] = product[:HALF].astype(BF16)
        remote(pair_out.at[t], pair_in.at[t], pair_sent, pair_sem.at[t], partner).start()
        own[lax.rem(t, 2)] = product[HALF:]

    def quarter(ref, q):
        return ref.at[pl.ds(pl.multiple_of(QUARTER * q, 16), QUARTER)]

    def chip_sum(t):
        await_bytes(pair_in.at[t], pair_sem.at[t])
        oy, oc, block = owner_of(t)
        mine = (own[lax.rem(t, 2)] + pair_in[t].astype(F32)).astype(BF16)
        away = lax.rem(y - oy + NY, NY)
        here = (away == 0) & (oc == c)
        owner = place(x, oy, z, oc)

        @pl.when(here)
        def _():
            sum_in[block, 0] = mine

        @pl.when(jnp.logical_not(here))
        def _():
            sum_out[t] = mine

        @pl.when((away == 0) & (oc != c))
        def _():
            remote(sum_out.at[t], sum_in.at[block, 1], sum_sent, sum_sem.at[block, 1, 0], owner).start()

        @pl.when(away == 2)
        def _():
            for q, step in enumerate((-1, 1)):
                remote(
                    quarter(sum_out.at[t], q), relay_in.at[t], sum_sent, relay_sem.at[t],
                    place(x, lax.rem(y + step + NY, NY), z, c),
                ).start()

        @pl.when(lax.rem(away, 2) == 1)
        def _():
            add_to_owner(t, 1 - away // 2)

    def add_to_owner(t, q):
        oy, oc, block = owner_of(t)
        away = lax.rem(y - oy + NY, NY)
        spot = 2 + 2 * (away // 2) + jnp.where(oc == c, 0, 1)
        remote(
            quarter(sum_out.at[t], q), quarter(sum_in.at[block, spot], q), sum_sent, sum_sem.at[block, spot, q],
            place(x, oy, z, oc),
        ).start()

    def relay_sum(t):
        oy, _, _ = owner_of(t)
        away = lax.rem(y - oy + NY, NY)

        @pl.when(lax.rem(away, 2) == 1)
        def _():
            await_bytes(relay_in.at[t], relay_sem.at[t])
            rows = pl.ds(pl.multiple_of(QUARTER * (away // 2), 16), QUARTER)
            sum_out[t, rows, :] = (sum_out[t, rows, :].astype(F32) + relay_in[t].astype(F32)).astype(BF16)
            add_to_owner(t, away // 2)

    def own_step(t):
        oy, oc, block = owner_of(t)

        @pl.when((oy == y) & (oc == c))
        def _():
            await_bytes(sum_in.at[block, 1], sum_sem.at[block, 1, 0])
            for spot in range(2, 6):
                for q in range(2):
                    await_bytes(quarter(sum_in.at[block, spot], q), sum_sem.at[block, spot, q])
            columns = pl.ds(pl.multiple_of(block * WIDE, WIDE), WIDE)
            for e in range(2):
                rows = pl.ds(pl.multiple_of(HALF * (c if e == 0 else 1 - c), 16), HALF)
                rotated = sum_in[block, e].astype(F32)
                for side in range(2):
                    rotated = rotated + sum_in[block, 2 + 2 * side + e].astype(F32)
                first_new = beta_one * first[rows, columns] + (1.0 - beta_one) * rotated
                second_new = beta_two * second[rows, columns] + (1.0 - beta_two) * rotated * rotated
                step = first_new / correct_one / (jnp.sqrt(second_new / correct_two) + adam_epsilon)
                first[rows, columns] = first_new
                second[rows, columns] = second_new
                steps[t, rows, :] = step.astype(BF16)
            for h in range(2):
                half = steps.at[t, pl.ds(HALF * h, HALF)]
                for k in (1, NY - 1):
                    remote(half, half, step_sent, near_sem.at[t], place(x, lax.rem(y + k, NY), z, h)).start()
            remote(steps.at[t], steps.at[t], step_sent, near_sem.at[t], partner).start()
            pltpu.make_async_copy(first.at[:, columns], first_out.at[:, columns], store_sem.at[0]).start()
            pltpu.make_async_copy(second.at[:, columns], second_out.at[:, columns], store_sem.at[1]).start()

    def my_half(t):
        return steps.at[t, pl.ds(pl.multiple_of(HALF * c, 16), HALF)]

    def pass_step(t):
        oy, _, _ = owner_of(t)
        away = lax.rem(y - oy + NY, NY)

        @pl.when(lax.rem(away, 2) == 1)
        def _():
            await_bytes(my_half(t), near_sem.at[t])
            q = away // 2
            part = quarter(my_half(t), q)
            remote(part, part, step_sent, quarter_sem.at[t, q], place(x, lax.rem(y + 1 + 2 * q, NY), z, c)).start()
            remote(my_half(t), my_half(t), step_sent, other_sem.at[t], partner).start()

    def pass_far(t):
        oy, _, _ = owner_of(t)

        @pl.when(lax.rem(y - oy + NY, NY) == 2)
        def _():
            for q in range(2):
                await_bytes(quarter(my_half(t), q), quarter_sem.at[t, q])
            remote(my_half(t), my_half(t), step_sent, other_sem.at[t], partner).start()

    def second_product(t):
        oy, oc, _ = owner_of(t)

        @pl.when(oy != y)
        def _():
            await_bytes(steps.at[t, pl.ds(0, HALF)], other_sem.at[t])

        @pl.when((oy == y) & (oc != c))
        def _():
            await_bytes(steps.at[t], near_sem.at[t])

        for k in range(ROWS // 256):
            rows = pl.ds(256 * k, 256)
            total[:, rows] += lax.dot_general(
                steps[t], panel[t, rows], (((1,), (1,)), ((), ())), preferred_element_type=F32
            )

    def body(t, carry):
        for group in range(0, CHUNKS, 8):

            @pl.when((t >= group) & (t < group + 8))
            def _():
                for slot in range(group, group + 8):
                    if ARRIVALS[slot]:

                        @pl.when(t == slot)
                        def _():
                            for part, i, j, half in ARRIVALS[slot]:
                                await_bytes(*chunk_piece(part, half, SLOT[i, j]))
                                for link, piece in onward(part, i, j, half):
                                    hand_on(part, i, j, link, piece)

        def stage(lag, work):
            @pl.when((t >= lag) & (t < CHUNKS + lag))
            def _():
                work(t - lag)

        stage(LAG_SUM, chip_sum)
        stage(0, first_product)
        stage(LAG_RELAY, relay_sum)
        stage(LAG_OWN, own_step)
        stage(LAG_PASS, pass_step)
        stage(LAG_FAR, pass_far)
        stage(LAG_UPDATE, second_product)
        return carry

    lax.fori_loop(0, CHUNKS + LAG_UPDATE, body, 0)

    stores = []
    for k in range(4):
        rows = pl.ds(256 * k, 256)
        update[:, rows] = total[:, rows].astype(BF16)
        stores.append(pltpu.make_async_copy(update.at[:, rows], update_hbm.at[:, rows], store_sem.at[2]))
        stores[-1].start()
    await_bytes(panel.at[pl.ds(1, CHUNKS - 1)], chunk_sent)
    await_bytes(pair_out, pair_sent)
    await_bytes(sum_out.at[pl.ds(0, CHUNKS - 4)], sum_sent)
    await_bytes(steps.at[pl.ds(0, CHUNKS - 4)], step_sent)
    await_bytes(first, store_sem.at[0])
    await_bytes(second, store_sem.at[1])
    await_bytes(update, store_sem.at[2])


def on_device(gradient, left_basis, first_moment, second_moment):
    dma = pltpu.SemaphoreType.DMA
    outs = pl.pallas_call(
        kernel,
        out_shape=(
            jax.ShapeDtypeStruct((COLS, ROWS), BF16),
            jax.ShapeDtypeStruct((COLS, ROWS), F32),
            jax.ShapeDtypeStruct((COLS, ROWS), F32),
        ),
        in_specs=[pl.BlockSpec(memory_space=pl.ANY)] * 4,
        out_specs=tuple([pl.BlockSpec(memory_space=pl.ANY)] * 3),
        scratch_shapes=[
            pltpu.VMEM((CHUNKS, ROWS, WIDE), BF16),
            pltpu.VMEM((COLS, ROWS), BF16),
            pltpu.VMEM((COLS, ROWS), BF16),
            pltpu.VMEM((COLS, ROWS), F32),
            pltpu.VMEM((COLS, ROWS), F32),
            pltpu.VMEM((2, HALF, WIDE), F32),
            pltpu.VMEM((CHUNKS, HALF, WIDE), BF16),
            pltpu.VMEM((CHUNKS, HALF, WIDE), BF16),
            pltpu.VMEM((CHUNKS, HALF, WIDE), BF16),
            pltpu.VMEM((CHUNKS, QUARTER, WIDE), BF16),
            pltpu.VMEM((4, 6, HALF, WIDE), BF16),
            pltpu.VMEM((CHUNKS, COLS, WIDE), BF16),
            pltpu.VMEM((COLS, ROWS), F32),
            pltpu.VMEM((COLS, ROWS), BF16),
            dma((4,)),
            dma((3,)),
            dma((CHUNKS, 4)),
            dma,
            dma((CHUNKS,)),
            dma,
            dma((CHUNKS,)),
            dma((4, 6, 2)),
            dma,
            dma((CHUNKS,)),
            dma((CHUNKS, 2)),
            dma((CHUNKS,)),
            dma,
        ],
        compiler_params=pltpu.CompilerParams(
            collective_id=0, has_side_effects=True, vmem_limit_bytes=60 << 20
        ),
        cost_estimate=pl.CostEstimate(flops=4 * 8192 * ROWS * COLS, bytes_accessed=10 << 20, transcendentals=0),
    )(gradient.T, left_basis, first_moment.T, second_moment.T)
    return tuple(out.T for out in outs)


def solution(mesh):
    placed = P("fsdp", ("tp", "layer"))
    return jax.shard_map(
        on_device, mesh=mesh, in_specs=(placed,) * 4, out_specs=(placed,) * 3, check_vma=False
    )
```

```python
import jax
import jax.numpy as jnp
from jax import lax
from jax.experimental import pallas as pl
from jax.experimental.pallas import tpu as pltpu
from jax.sharding import PartitionSpec as P

STEP = 20


beta_one = 0.9
beta_two = 0.95
adam_epsilon = 1e-08
correct_one = 1.0 - beta_one**STEP
correct_two = 1.0 - beta_two**STEP

MESH = pl.DeviceIdType.MESH
BF16 = jnp.bfloat16
F32 = jnp.float32

ROWS, COLS, WIDE = 1024, 448, 256
HALF = COLS // 2
QUARTER = HALF // 2
NX, NY, NZ = 4, 4, 8
CHUNKS = NX * NZ

PART_P = 608
SPANS = {
    ("P", "F"): (0, PART_P),
    ("P", "A"): (0, PART_P // 2),
    ("P", "B"): (PART_P // 2, PART_P // 2),
    ("Q", "F"): (PART_P, ROWS - PART_P),
    ("Q", "A"): (PART_P, (ROWS - PART_P) // 2),
    ("Q", "B"): ((PART_P + ROWS) // 2, (ROWS - PART_P) // 2),
}
ORDER = (
    (0, 0), (-1, 0), (1, 0), (0, -1), (0, 1), (-1, -1), (1, -1), (-1, 1), (1, 1), (2, 0), (0, -2), (0, 2), (2, -1), (2, 1), (-1, -2), (1, -2), (-1, 2), (1, 2), (0, -3), (0, 3), (2, -2), (2, 2), (-1, -3), (1, -3), (-1, 3), (1, 3), (0, 4), (2, -3), (2, 3), (-1, 4), (1, 4), (2, 4),
)
ARRIVALS = (
    (),
    (("Q", -1, 0, "F"), ("Q", 1, 0, "F"), ("P", 0, -1, "F"), ("P", 0, 1, "F"), ("P", -1, 0, "F"), ("P", 1, 0, "F"), ("Q", 0, -1, "F"), ("Q", 0, 1, "F"),),
    (("Q", 2, 0, "A"), ("Q", 2, 0, "B"),),
    (("Q", -1, -1, "F"), ("Q", -1, 1, "F"),),
    (),
    (("P", -1, -1, "F"), ("P", 1, -1, "F"), ("Q", 1, -1, "F"), ("Q", 1, 1, "F"),),
    (),
    (("P", -1, 1, "F"), ("P", 1, 1, "F"), ("P", 0, -2, "F"), ("P", 0, 2, "F"),),
    (),
    (("P", 2, 0, "A"), ("P", 2, 0, "B"), ("Q", 0, -2, "F"), ("Q", 0, 2, "F"),),
    (("P", 2, -1, "A"), ("P", 2, -1, "B"), ("Q", 2, -1, "A"), ("Q", 2, 1, "A"),),
    (("Q", 2, -1, "B"), ("Q", 2, 1, "B"), ("P", 2, 1, "A"), ("P", 2, 1, "B"),),
    (),
    (("Q", -1, -2, "F"), ("Q", -1, 2, "F"),),
    (("P", -1, -2, "F"), ("P", 1, -2, "F"),),
    (("Q", 1, -2, "F"), ("Q", 1, 2, "F"),),
    (("P", -1, 2, "F"), ("P", 1, 2, "F"),),
    (("P", 0, -3, "F"), ("P", 0, 3, "F"),),
    (("P", 2, -2, "A"), ("P", 2, -2, "B"), ("Q", 0, -3, "F"), ("Q", 0, 3, "F"),),
    (("P", 2, 2, "A"), ("P", 2, 2, "B"), ("Q", 2, -2, "A"), ("Q", 2, 2, "A"),),
    (("Q", 2, -2, "B"), ("Q", 2, 2, "B"),),
    (("P", -1, -3, "F"), ("P", 1, -3, "F"),),
    (("Q", -1, -3, "F"), ("Q", -1, 3, "F"),),
    (("Q", 1, -3, "F"), ("Q", 1, 3, "F"), ("P", -1, 3, "F"), ("P", 1, 3, "F"),),
    (),
    (("P", 0, 4, "A"), ("P", 0, 4, "B"), ("P", 2, -3, "A"), ("P", 2, -3, "B"),),
    (("Q", 0, 4, "A"), ("Q", 0, 4, "B"), ("P", 2, 3, "A"), ("P", 2, 3, "B"),),
    (("Q", 2, -3, "A"), ("Q", 2, 3, "A"), ("Q", 2, -3, "B"), ("Q", 2, 3, "B"), ("P", -1, 4, "A"), ("P", 1, 4, "A"),),
    (("Q", -1, 4, "A"), ("Q", -1, 4, "B"),),
    (("P", -1, 4, "B"), ("P", 1, 4, "B"), ("Q", 1, 4, "A"), ("Q", 1, 4, "B"),),
    (("P", 2, 4, "A"), ("Q", 2, 4, "A"), ("Q", 2, 4, "B"),),
    (("P", 2, 4, "B"),),
)
SLOT = {offset: slot for slot, offset in enumerate(ORDER)}

LAG_SUM, LAG_RELAY, LAG_OWN, LAG_PASS, LAG_FAR, LAG_UPDATE = 1, 3, 7, 10, 13, 15


def bits(values, shift):
    word = sum((((value >> shift) & 1) << k) for k, value in enumerate(values))
    return word - (1 << 32) if word >= 1 << 31 else word


X_BITS = [bits([i % NX for i, _ in ORDER], s) for s in range(2)]
Z_BITS = [bits([j % NZ for _, j in ORDER], s) for s in range(3)]


def lookup(words, t):
    total = 0
    for s, word in enumerate(words):
        total = total + (lax.shift_right_logical(jnp.int32(word), t) & 1) * (1 << s)
    return total


def onward(part, i, j, half):
    out = []
    if part == "P":
        if i == 0:
            if j == 0:
                out += [("z+", "F"), ("z-", "F")]
            elif j in (-1, -2):
                out += [("z+", "F")]
            elif j in (1, 2):
                out += [("z-", "F")]
            elif j == -3:
                out += [("z+", "A")]
            elif j == 3:
                out += [("z-", "B")]
            out += [("x+", half), ("x-", half)]
        elif i == -1 and half in "FA":
            out += [("x+", "A")]
        elif i == 1 and half in "FB":
            out += [("x-", "B")]
    elif j == 0:
        if i == 0:
            out += [("x+", "F"), ("x-", "F")]
        elif i == -1:
            out += [("x+", "A")]
        elif i == 1:
            out += [("x-", "B")]
        out += [("z+", half), ("z-", half)]
    elif j in (-1, -2):
        out += [("z+", half)]
    elif j in (1, 2):
        out += [("z-", half)]
    elif j == -3 and half in "FA":
        out += [("z+", "A")]
    elif j == 3 and half in "FB":
        out += [("z-", "B")]
    return out


def seen_from(link, i, j):
    i += {"x+": -1, "x-": 1}.get(link, 0)
    j += {"z+": -1, "z-": 1}.get(link, 0)
    return (i + 1) % NX - 1, (j + 3) % NZ - 3


def kernel(
    grad_hbm, basis_hbm, first_hbm, second_hbm,
    update_hbm, first_out, second_out,
    panel, grad, grad_t, first, second, own, pair_out, pair_in, sum_out, relay_in, sum_in, steps, total, update,
    load_sem, store_sem, chunk_sem, chunk_sent, pair_sem, pair_sent, relay_sem, sum_sem, sum_sent, near_sem, quarter_sem, other_sem, step_sent,
):
    f, tp, layer = lax.axis_index("fsdp"), lax.axis_index("tp"), lax.axis_index("layer")
    x, y, z, c = layer * 2 + tp // NZ, f // 2, tp % NZ, f % 2

    def place(px, py, pz, pc):
        return (py * 2 + pc, (px % 2) * NZ + pz, px // 2)

    partner = place(x, y, z, 1 - c)
    neighbours = {
        "x+": place((x + 1) % NX, y, z, c),
        "x-": place((x + NX - 1) % NX, y, z, c),
        "z+": place(x, y, (z + 1) % NZ, c),
        "z-": place(x, y, (z + NZ - 1) % NZ, c),
    }

    def remote(source, target, send_sem, recv_sem, device):
        return pltpu.make_async_remote_copy(
            src_ref=source, dst_ref=target, send_sem=send_sem, recv_sem=recv_sem, device_id=device, device_id_type=MESH
        )

    def await_bytes(ref, sem):
        pltpu.make_async_copy(ref, ref, sem).wait()

    loads = [
        pltpu.make_async_copy(basis_hbm, panel.at[0], load_sem.at[0]),
        pltpu.make_async_copy(grad_hbm, grad, load_sem.at[1]),
        pltpu.make_async_copy(first_hbm, first, load_sem.at[2]),
        pltpu.make_async_copy(second_hbm, second, load_sem.at[3]),
    ]
    for load in loads:
        load.start()

    barrier = pltpu.get_barrier_semaphore()
    peers = list(neighbours.values()) + [partner]
    for k in range(1, NY):
        for pc in range(2):
            peers.append(place(x, (y + k) % NY, z, pc))
    for peer in peers:
        pl.semaphore_signal(barrier, inc=1, device_id=peer, device_id_type=MESH)
    loads[0].wait()
    pl.semaphore_wait(barrier, len(peers))

    def chunk_piece(part, half, slot):
        start, size = SPANS[part, half]
        return panel.at[slot, pl.ds(start, size)], chunk_sem.at[slot, 2 * (part == "Q") + (half == "B")]

    def hand_on(part, i, j, link, half):
        start, size = SPANS[part, half]
        target, sem = chunk_piece(part, half, SLOT[seen_from(link, i, j)])
        remote(panel.at[SLOT[i, j], pl.ds(start, size)], target, chunk_sent, sem, neighbours[link]).start()

    for link in ("x+", "x-"):
        hand_on("Q", 0, 0, link, "F")
    for link in ("z+", "z-"):
        hand_on("P", 0, 0, link, "F")
    for link in ("x+", "x-"):
        hand_on("P", 0, 0, link, "F")
    for link in ("z+", "z-"):
        hand_on("Q", 0, 0, link, "F")

    loads[1].wait()
    for h in range(2):
        at = pl.multiple_of(jnp.where(c == h, HALF, 0), 16)
        grad_t[pl.ds(at, HALF), :] = grad[pl.ds(HALF * h, HALF), :]
    total[...] = jnp.zeros_like(total)
    loads[2].wait()
    loads[3].wait()

    def owner_of(t):
        xs, zs = lax.rem(x + lookup(X_BITS, t), NX), lax.rem(z + lookup(Z_BITS, t), NZ)
        return 2 * lax.rem(xs, 2) + zs // 4, lax.rem(zs // 2, 2), 2 * lax.rem(zs, 2) + xs // 2

    def first_product(t):
        product = jnp.dot(grad_t[...], panel[t], preferred_element_type=F32)
        pair_out[t] = product[:HALF].astype(BF16)
        remote(pair_out.at[t], pair_in.at[t], pair_sent, pair_sem.at[t], partner).start()
        own[lax.rem(t, 2)] = product[HALF:]

    def quarter(ref, q):
        return ref.at[pl.ds(pl.multiple_of(QUARTER * q, 16), QUARTER)]

    def chip_sum(t):
        await_bytes(pair_in.at[t], pair_sem.at[t])
        oy, oc, block = owner_of(t)
        mine = (own[lax.rem(t, 2)] + pair_in[t].astype(F32)).astype(BF16)
        away = lax.rem(y - oy + NY, NY)
        here = (away == 0) & (oc == c)
        owner = place(x, oy, z, oc)

        @pl.when(here)
        def _():
            sum_in[block, 0] = mine

        @pl.when(jnp.logical_not(here))
        def _():
            sum_out[t] = mine

        @pl.when((away == 0) & (oc != c))
        def _():
            remote(sum_out.at[t], sum_in.at[block, 1], sum_sent, sum_sem.at[block, 1, 0], owner).start()

        @pl.when(away == 2)
        def _():
            for q, step in enumerate((-1, 1)):
                remote(
                    quarter(sum_out.at[t], q), relay_in.at[t], sum_sent, relay_sem.at[t],
                    place(x, lax.rem(y + step + NY, NY), z, c),
                ).start()

        @pl.when(lax.rem(away, 2) == 1)
        def _():
            add_to_owner(t, 1 - away // 2)

    def add_to_owner(t, q):
        oy, oc, block = owner_of(t)
        away = lax.rem(y - oy + NY, NY)
        spot = 2 + 2 * (away // 2) + jnp.where(oc == c, 0, 1)
        remote(
            quarter(sum_out.at[t], q), quarter(sum_in.at[block, spot], q), sum_sent, sum_sem.at[block, spot, q],
            place(x, oy, z, oc),
        ).start()

    def relay_sum(t):
        oy, _, _ = owner_of(t)
        away = lax.rem(y - oy + NY, NY)

        @pl.when(lax.rem(away, 2) == 1)
        def _():
            await_bytes(relay_in.at[t], relay_sem.at[t])
            rows = pl.ds(pl.multiple_of(QUARTER * (away // 2), 16), QUARTER)
            sum_out[t, rows, :] = (sum_out[t, rows, :].astype(F32) + relay_in[t].astype(F32)).astype(BF16)
            add_to_owner(t, away // 2)

    def own_step(t):
        oy, oc, block = owner_of(t)

        @pl.when((oy == y) & (oc == c))
        def _():
            await_bytes(sum_in.at[block, 1], sum_sem.at[block, 1, 0])
            for spot in range(2, 6):
                for q in range(2):
                    await_bytes(quarter(sum_in.at[block, spot], q), sum_sem.at[block, spot, q])
            columns = pl.ds(pl.multiple_of(block * WIDE, WIDE), WIDE)
            for e in range(2):
                rows = pl.ds(pl.multiple_of(HALF * (c if e == 0 else 1 - c), 16), HALF)
                rotated = sum_in[block, e].astype(F32)
                for side in range(2):
                    rotated = rotated + sum_in[block, 2 + 2 * side + e].astype(F32)
                first_new = beta_one * first[rows, columns] + (1.0 - beta_one) * rotated
                second_new = beta_two * second[rows, columns] + (1.0 - beta_two) * rotated * rotated
                step = first_new / correct_one / (jnp.sqrt(second_new / correct_two) + adam_epsilon)
                first[rows, columns] = first_new
                second[rows, columns] = second_new
                steps[t, rows, :] = step.astype(BF16)
            for h in range(2):
                half = steps.at[t, pl.ds(HALF * h, HALF)]
                for k in (1, NY - 1):
                    remote(half, half, step_sent, near_sem.at[t], place(x, lax.rem(y + k, NY), z, h)).start()
            remote(steps.at[t], steps.at[t], step_sent, near_sem.at[t], partner).start()
            pltpu.make_async_copy(first.at[:, columns], first_out.at[:, columns], store_sem.at[0]).start()
            pltpu.make_async_copy(second.at[:, columns], second_out.at[:, columns], store_sem.at[1]).start()

    def my_half(t):
        return steps.at[t, pl.ds(pl.multiple_of(HALF * c, 16), HALF)]

    def pass_step(t):
        oy, _, _ = owner_of(t)
        away = lax.rem(y - oy + NY, NY)

        @pl.when(lax.rem(away, 2) == 1)
        def _():
            await_bytes(my_half(t), near_sem.at[t])
            q = away // 2
            part = quarter(my_half(t), q)
            remote(part, part, step_sent, quarter_sem.at[t, q], place(x, lax.rem(y + 1 + 2 * q, NY), z, c)).start()
            remote(my_half(t), my_half(t), step_sent, other_sem.at[t], partner).start()

    def pass_far(t):
        oy, _, _ = owner_of(t)

        @pl.when(lax.rem(y - oy + NY, NY) == 2)
        def _():
            for q in range(2):
                await_bytes(quarter(my_half(t), q), quarter_sem.at[t, q])
            remote(my_half(t), my_half(t), step_sent, other_sem.at[t], partner).start()

    def second_product(t):
        oy, oc, _ = owner_of(t)

        @pl.when(oy != y)
        def _():
            await_bytes(steps.at[t, pl.ds(0, HALF)], other_sem.at[t])

        @pl.when((oy == y) & (oc != c))
        def _():
            await_bytes(steps.at[t], near_sem.at[t])

        for k in range(ROWS // 256):
            rows = pl.ds(256 * k, 256)
            total[:, rows] += lax.dot_general(
                steps[t], panel[t, rows], (((1,), (1,)), ((), ())), preferred_element_type=F32
            )

    def body(t, carry):
        for group in range(0, CHUNKS, 8):

            @pl.when((t >= group) & (t < group + 8))
            def _():
                for slot in range(group, group + 8):
                    if ARRIVALS[slot]:

                        @pl.when(t == slot)
                        def _():
                            for part, i, j, half in ARRIVALS[slot]:
                                await_bytes(*chunk_piece(part, half, SLOT[i, j]))
                                for link, piece in onward(part, i, j, half):
                                    hand_on(part, i, j, link, piece)

        def stage(lag, work):
            @pl.when((t >= lag) & (t < CHUNKS + lag))
            def _():
                work(t - lag)

        stage(LAG_SUM, chip_sum)
        stage(0, first_product)
        stage(LAG_RELAY, relay_sum)
        stage(LAG_OWN, own_step)
        stage(LAG_PASS, pass_step)
        stage(LAG_FAR, pass_far)
        stage(LAG_UPDATE, second_product)
        return carry

    lax.fori_loop(0, CHUNKS + LAG_UPDATE, body, 0)

    stores = []
    for k in range(4):
        rows = pl.ds(256 * k, 256)
        update[:, rows] = total[:, rows].astype(BF16)
        stores.append(pltpu.make_async_copy(update.at[:, rows], update_hbm.at[:, rows], store_sem.at[2]))
        stores[-1].start()
    await_bytes(panel.at[pl.ds(1, CHUNKS - 1)], chunk_sent)
    await_bytes(pair_out, pair_sent)
    await_bytes(sum_out.at[pl.ds(0, CHUNKS - 4)], sum_sent)
    await_bytes(steps.at[pl.ds(0, CHUNKS - 4)], step_sent)
    await_bytes(first, store_sem.at[0])
    await_bytes(second, store_sem.at[1])
    await_bytes(update, store_sem.at[2])


def on_device(gradient, left_basis, first_moment, second_moment):
    dma = pltpu.SemaphoreType.DMA
    outs = pl.pallas_call(
        kernel,
        out_shape=(
            jax.ShapeDtypeStruct((COLS, ROWS), BF16),
            jax.ShapeDtypeStruct((COLS, ROWS), F32),
            jax.ShapeDtypeStruct((COLS, ROWS), F32),
        ),
        in_specs=[pl.BlockSpec(memory_space=pl.ANY)] * 4,
        out_specs=tuple([pl.BlockSpec(memory_space=pl.ANY)] * 3),
        scratch_shapes=[
            pltpu.VMEM((CHUNKS, ROWS, WIDE), BF16),
            pltpu.VMEM((COLS, ROWS), BF16),
            pltpu.VMEM((COLS, ROWS), BF16),
            pltpu.VMEM((COLS, ROWS), F32),
            pltpu.VMEM((COLS, ROWS), F32),
            pltpu.VMEM((2, HALF, WIDE), F32),
            pltpu.VMEM((CHUNKS, HALF, WIDE), BF16),
            pltpu.VMEM((CHUNKS, HALF, WIDE), BF16),
            pltpu.VMEM((CHUNKS, HALF, WIDE), BF16),
            pltpu.VMEM((CHUNKS, QUARTER, WIDE), BF16),
            pltpu.VMEM((4, 6, HALF, WIDE), BF16),
            pltpu.VMEM((CHUNKS, COLS, WIDE), BF16),
            pltpu.VMEM((COLS, ROWS), F32),
            pltpu.VMEM((COLS, ROWS), BF16),
            dma((4,)),
            dma((3,)),
            dma((CHUNKS, 4)),
            dma,
            dma((CHUNKS,)),
            dma,
            dma((CHUNKS,)),
            dma((4, 6, 2)),
            dma,
            dma((CHUNKS,)),
            dma((CHUNKS, 2)),
            dma((CHUNKS,)),
            dma,
        ],
        compiler_params=pltpu.CompilerParams(
            collective_id=0, has_side_effects=True, vmem_limit_bytes=60 << 20
        ),
        cost_estimate=pl.CostEstimate(flops=4 * 8192 * ROWS * COLS, bytes_accessed=10 << 20, transcendentals=0),
    )(gradient.T, left_basis, first_moment.T, second_moment.T)
    return tuple(out.T for out in outs)


def solution(mesh):
    placed = P("fsdp", ("tp", "layer"))
    return jax.shard_map(
        on_device, mesh=mesh, in_specs=(placed,) * 4, out_specs=(placed,) * 3, check_vma=False
    )
```

```python
import jax
import jax.numpy as jnp
from jax import lax
from jax.experimental import pallas as pl
from jax.experimental.pallas import tpu as pltpu
from jax.sharding import PartitionSpec as P

STEP = 20


beta_one = 0.9
beta_two = 0.95
adam_epsilon = 1e-08
correct_one = 1.0 - beta_one**STEP
correct_two = 1.0 - beta_two**STEP

MESH = pl.DeviceIdType.MESH
BF16 = jnp.bfloat16
F32 = jnp.float32

ROWS, COLS, WIDE = 1024, 448, 256
HALF = COLS // 2
QUARTER = HALF // 2
NX, NY, NZ = 4, 4, 8
CHUNKS = NX * NZ

PART_P = 608
SPANS = {
    ("P", "F"): (0, PART_P),
    ("P", "A"): (0, PART_P // 2),
    ("P", "B"): (PART_P // 2, PART_P // 2),
    ("Q", "F"): (PART_P, ROWS - PART_P),
    ("Q", "A"): (PART_P, (ROWS - PART_P) // 2),
    ("Q", "B"): ((PART_P + ROWS) // 2, (ROWS - PART_P) // 2),
}
ORDER = (
    (0, 0), (-1, 0), (1, 0), (0, -1), (0, 1), (-1, -1), (1, -1), (-1, 1), (1, 1), (2, 0), (0, -2), (0, 2), (2, -1), (2, 1), (-1, -2), (1, -2), (-1, 2), (1, 2), (0, -3), (0, 3), (2, -2), (2, 2), (-1, -3), (1, -3), (-1, 3), (1, 3), (0, 4), (2, -3), (2, 3), (-1, 4), (1, 4), (2, 4),
)
ARRIVALS = (
    (),
    (("Q", -1, 0, "F"), ("Q", 1, 0, "F"), ("P", 0, -1, "F"), ("P", 0, 1, "F"), ("P", -1, 0, "F"), ("P", 1, 0, "F"), ("Q", 0, -1, "F"), ("Q", 0, 1, "F"),),
    (("Q", 2, 0, "A"), ("Q", 2, 0, "B"),),
    (("Q", -1, -1, "F"), ("Q", -1, 1, "F"),),
    (),
    (("P", -1, -1, "F"), ("P", 1, -1, "F"), ("Q", 1, -1, "F"), ("Q", 1, 1, "F"),),
    (),
    (("P", -1, 1, "F"), ("P", 1, 1, "F"), ("P", 0, -2, "F"), ("P", 0, 2, "F"),),
    (),
    (("P", 2, 0, "A"), ("P", 2, 0, "B"), ("Q", 0, -2, "F"), ("Q", 0, 2, "F"),),
    (("P", 2, -1, "A"), ("P", 2, -1, "B"), ("Q", 2, -1, "A"), ("Q", 2, 1, "A"),),
    (("Q", 2, -1, "B"), ("Q", 2, 1, "B"), ("P", 2, 1, "A"), ("P", 2, 1, "B"),),
    (),
    (("Q", -1, -2, "F"), ("Q", -1, 2, "F"),),
    (("P", -1, -2, "F"), ("P", 1, -2, "F"),),
    (("Q", 1, -2, "F"), ("Q", 1, 2, "F"),),
    (("P", -1, 2, "F"), ("P", 1, 2, "F"),),
    (("P", 0, -3, "F"), ("P", 0, 3, "F"),),
    (("P", 2, -2, "A"), ("P", 2, -2, "B"), ("Q", 0, -3, "F"), ("Q", 0, 3, "F"),),
    (("P", 2, 2, "A"), ("P", 2, 2, "B"), ("Q", 2, -2, "A"), ("Q", 2, 2, "A"),),
    (("Q", 2, -2, "B"), ("Q", 2, 2, "B"),),
    (("P", -1, -3, "F"), ("P", 1, -3, "F"),),
    (("Q", -1, -3, "F"), ("Q", -1, 3, "F"),),
    (("Q", 1, -3, "F"), ("Q", 1, 3, "F"), ("P", -1, 3, "F"), ("P", 1, 3, "F"),),
    (),
    (("P", 0, 4, "A"), ("P", 0, 4, "B"), ("P", 2, -3, "A"), ("P", 2, -3, "B"),),
    (("Q", 0, 4, "A"), ("Q", 0, 4, "B"), ("P", 2, 3, "A"), ("P", 2, 3, "B"),),
    (("Q", 2, -3, "A"), ("Q", 2, 3, "A"), ("Q", 2, -3, "B"), ("Q", 2, 3, "B"), ("P", -1, 4, "A"), ("P", 1, 4, "A"),),
    (("Q", -1, 4, "A"), ("Q", -1, 4, "B"),),
    (("P", -1, 4, "B"), ("P", 1, 4, "B"), ("Q", 1, 4, "A"), ("Q", 1, 4, "B"),),
    (("P", 2, 4, "A"), ("Q", 2, 4, "A"), ("Q", 2, 4, "B"),),
    (("P", 2, 4, "B"),),
)
SLOT = {offset: slot for slot, offset in enumerate(ORDER)}

LAG_SUM, LAG_RELAY, LAG_OWN, LAG_PASS, LAG_FAR, LAG_UPDATE = 1, 3, 7, 10, 13, 15


def bits(values, shift):
    word = sum((((value >> shift) & 1) << k) for k, value in enumerate(values))
    return word - (1 << 32) if word >= 1 << 31 else word


X_BITS = [bits([i % NX for i, _ in ORDER], s) for s in range(2)]
Z_BITS = [bits([j % NZ for _, j in ORDER], s) for s in range(3)]


def lookup(words, t):
    total = 0
    for s, word in enumerate(words):
        total = total + (lax.shift_right_logical(jnp.int32(word), t) & 1) * (1 << s)
    return total


def onward(part, i, j, half):
    out = []
    if part == "P":
        if i == 0:
            if j == 0:
                out += [("z+", "F"), ("z-", "F")]
            elif j in (-1, -2):
                out += [("z+", "F")]
            elif j in (1, 2):
                out += [("z-", "F")]
            elif j == -3:
                out += [("z+", "A")]
            elif j == 3:
                out += [("z-", "B")]
            out += [("x+", half), ("x-", half)]
        elif i == -1 and half in "FA":
            out += [("x+", "A")]
        elif i == 1 and half in "FB":
            out += [("x-", "B")]
    elif j == 0:
        if i == 0:
            out += [("x+", "F"), ("x-", "F")]
        elif i == -1:
            out += [("x+", "A")]
        elif i == 1:
            out += [("x-", "B")]
        out += [("z+", half), ("z-", half)]
    elif j in (-1, -2):
        out += [("z+", half)]
    elif j in (1, 2):
        out += [("z-", half)]
    elif j == -3 and half in "FA":
        out += [("z+", "A")]
    elif j == 3 and half in "FB":
        out += [("z-", "B")]
    return out


def seen_from(link, i, j):
    i += {"x+": -1, "x-": 1}.get(link, 0)
    j += {"z+": -1, "z-": 1}.get(link, 0)
    return (i + 1) % NX - 1, (j + 3) % NZ - 3


def kernel(
    grad_hbm, basis_hbm, first_hbm, second_hbm,
    update_hbm, first_out, second_out,
    panel, grad, grad_t, first, second, own, pair_out, pair_in, sum_out, relay_in, sum_in, steps, total, update,
    load_sem, store_sem, chunk_sem, chunk_sent, pair_sem, pair_sent, relay_sem, sum_sem, sum_sent, near_sem, quarter_sem, other_sem, step_sent,
):
    f, tp, layer = lax.axis_index("fsdp"), lax.axis_index("tp"), lax.axis_index("layer")
    x, y, z, c = layer * 2 + tp // NZ, f // 2, tp % NZ, f % 2

    def place(px, py, pz, pc):
        return (py * 2 + pc, (px % 2) * NZ + pz, px // 2)

    partner = place(x, y, z, 1 - c)
    neighbours = {
        "x+": place((x + 1) % NX, y, z, c),
        "x-": place((x + NX - 1) % NX, y, z, c),
        "z+": place(x, y, (z + 1) % NZ, c),
        "z-": place(x, y, (z + NZ - 1) % NZ, c),
    }

    def remote(source, target, send_sem, recv_sem, device):
        return pltpu.make_async_remote_copy(
            src_ref=source, dst_ref=target, send_sem=send_sem, recv_sem=recv_sem, device_id=device, device_id_type=MESH
        )

    def await_bytes(ref, sem):
        pltpu.make_async_copy(ref, ref, sem).wait()

    loads = [
        pltpu.make_async_copy(basis_hbm, panel.at[0], load_sem.at[0]),
        pltpu.make_async_copy(grad_hbm, grad, load_sem.at[1]),
        pltpu.make_async_copy(first_hbm, first, load_sem.at[2]),
        pltpu.make_async_copy(second_hbm, second, load_sem.at[3]),
    ]
    for load in loads:
        load.start()

    barrier = pltpu.get_barrier_semaphore()
    peers = list(neighbours.values()) + [partner]
    for k in range(1, NY):
        for pc in range(2):
            peers.append(place(x, (y + k) % NY, z, pc))
    for peer in peers:
        pl.semaphore_signal(barrier, inc=1, device_id=peer, device_id_type=MESH)
    loads[0].wait()
    pl.semaphore_wait(barrier, len(peers))

    def chunk_piece(part, half, slot):
        start, size = SPANS[part, half]
        return panel.at[slot, pl.ds(start, size)], chunk_sem.at[slot, 2 * (part == "Q") + (half == "B")]

    def hand_on(part, i, j, link, half):
        start, size = SPANS[part, half]
        target, sem = chunk_piece(part, half, SLOT[seen_from(link, i, j)])
        remote(panel.at[SLOT[i, j], pl.ds(start, size)], target, chunk_sent, sem, neighbours[link]).start()

    for link in ("x+", "x-"):
        hand_on("Q", 0, 0, link, "F")
    for link in ("z+", "z-"):
        hand_on("P", 0, 0, link, "F")
    for link in ("x+", "x-"):
        hand_on("P", 0, 0, link, "F")
    for link in ("z+", "z-"):
        hand_on("Q", 0, 0, link, "F")

    loads[1].wait()
    for h in range(2):
        at = pl.multiple_of(jnp.where(c == h, HALF, 0), 16)
        grad_t[pl.ds(at, HALF), :] = grad[pl.ds(HALF * h, HALF), :]
    total[...] = jnp.zeros_like(total)
    loads[2].wait()
    loads[3].wait()

    def owner_of(t):
        xs, zs = lax.rem(x + lookup(X_BITS, t), NX), lax.rem(z + lookup(Z_BITS, t), NZ)
        return 2 * lax.rem(xs, 2) + zs // 4, lax.rem(zs // 2, 2), 2 * lax.rem(zs, 2) + xs // 2

    def first_product(t):
        product = jnp.dot(grad_t[...], panel[t], preferred_element_type=F32)
        pair_out[t] = product[:HALF].astype(BF16)
        remote(pair_out.at[t], pair_in.at[t], pair_sent, pair_sem.at[t], partner).start()
        own[lax.rem(t, 2)] = product[HALF:]

    def quarter(ref, q):
        return ref.at[pl.ds(pl.multiple_of(QUARTER * q, 16), QUARTER)]

    def chip_sum(t):
        await_bytes(pair_in.at[t], pair_sem.at[t])
        oy, oc, block = owner_of(t)
        mine = (own[lax.rem(t, 2)] + pair_in[t].astype(F32)).astype(BF16)
        away = lax.rem(y - oy + NY, NY)
        here = (away == 0) & (oc == c)
        owner = place(x, oy, z, oc)

        @pl.when(here)
        def _():
            sum_in[block, 0] = mine

        @pl.when(jnp.logical_not(here))
        def _():
            sum_out[t] = mine

        @pl.when((away == 0) & (oc != c))
        def _():
            remote(sum_out.at[t], sum_in.at[block, 1], sum_sent, sum_sem.at[block, 1, 0], owner).start()

        @pl.when(away == 2)
        def _():
            for q, step in enumerate((-1, 1)):
                remote(
                    quarter(sum_out.at[t], q), relay_in.at[t], sum_sent, relay_sem.at[t],
                    place(x, lax.rem(y + step + NY, NY), z, c),
                ).start()

        @pl.when(lax.rem(away, 2) == 1)
        def _():
            add_to_owner(t, 1 - away // 2)

    def add_to_owner(t, q):
        oy, oc, block = owner_of(t)
        away = lax.rem(y - oy + NY, NY)
        spot = 2 + 2 * (away // 2) + jnp.where(oc == c, 0, 1)
        remote(
            quarter(sum_out.at[t], q), quarter(sum_in.at[block, spot], q), sum_sent, sum_sem.at[block, spot, q],
            place(x, oy, z, oc),
        ).start()

    def relay_sum(t):
        oy, _, _ = owner_of(t)
        away = lax.rem(y - oy + NY, NY)

        @pl.when(lax.rem(away, 2) == 1)
        def _():
            await_bytes(relay_in.at[t], relay_sem.at[t])
            rows = pl.ds(pl.multiple_of(QUARTER * (away // 2), 16), QUARTER)
            sum_out[t, rows, :] = (sum_out[t, rows, :].astype(F32) + relay_in[t].astype(F32)).astype(BF16)
            add_to_owner(t, away // 2)

    def own_step(t):
        oy, oc, block = owner_of(t)

        @pl.when((oy == y) & (oc == c))
        def _():
            await_bytes(sum_in.at[block, 1], sum_sem.at[block, 1, 0])
            for spot in range(2, 6):
                for q in range(2):
                    await_bytes(quarter(sum_in.at[block, spot], q), sum_sem.at[block, spot, q])
            columns = pl.ds(pl.multiple_of(block * WIDE, WIDE), WIDE)
            for e in range(2):
                rows = pl.ds(pl.multiple_of(HALF * (c if e == 0 else 1 - c), 16), HALF)
                rotated = sum_in[block, e].astype(F32)
                for side in range(2):
                    rotated = rotated + sum_in[block, 2 + 2 * side + e].astype(F32)
                first_new = beta_one * first[rows, columns] + (1.0 - beta_one) * rotated
                second_new = beta_two * second[rows, columns] + (1.0 - beta_two) * rotated * rotated
                step = first_new / correct_one / (jnp.sqrt(second_new / correct_two) + adam_epsilon)
                first[rows, columns] = first_new
                second[rows, columns] = second_new
                steps[t, rows, :] = step.astype(BF16)
            for h in range(2):
                half = steps.at[t, pl.ds(HALF * h, HALF)]
                for k in (1, NY - 1):
                    remote(half, half, step_sent, near_sem.at[t], place(x, lax.rem(y + k, NY), z, h)).start()
            remote(steps.at[t], steps.at[t], step_sent, near_sem.at[t], partner).start()
            pltpu.make_async_copy(first.at[:, columns], first_out.at[:, columns], store_sem.at[0]).start()
            pltpu.make_async_copy(second.at[:, columns], second_out.at[:, columns], store_sem.at[1]).start()

    def my_half(t):
        return steps.at[t, pl.ds(pl.multiple_of(HALF * c, 16), HALF)]

    def pass_step(t):
        oy, _, _ = owner_of(t)
        away = lax.rem(y - oy + NY, NY)

        @pl.when(lax.rem(away, 2) == 1)
        def _():
            await_bytes(my_half(t), near_sem.at[t])
            q = away // 2
            part = quarter(my_half(t), q)
            remote(part, part, step_sent, quarter_sem.at[t, q], place(x, lax.rem(y + 1 + 2 * q, NY), z, c)).start()
            remote(my_half(t), my_half(t), step_sent, other_sem.at[t], partner).start()

    def pass_far(t):
        oy, _, _ = owner_of(t)

        @pl.when(lax.rem(y - oy + NY, NY) == 2)
        def _():
            for q in range(2):
                await_bytes(quarter(my_half(t), q), quarter_sem.at[t, q])
            remote(my_half(t), my_half(t), step_sent, other_sem.at[t], partner).start()

    def second_product(t):
        oy, oc, _ = owner_of(t)

        @pl.when(oy != y)
        def _():
            await_bytes(steps.at[t, pl.ds(0, HALF)], other_sem.at[t])

        @pl.when((oy == y) & (oc != c))
        def _():
            await_bytes(steps.at[t], near_sem.at[t])

        for k in range(ROWS // 256):
            rows = pl.ds(256 * k, 256)
            total[:, rows] += lax.dot_general(
                steps[t], panel[t, rows], (((1,), (1,)), ((), ())), preferred_element_type=F32
            )

    def body(t, carry):
        for group in range(0, CHUNKS, 8):

            @pl.when((t >= group) & (t < group + 8))
            def _():
                for slot in range(group, group + 8):
                    if ARRIVALS[slot]:

                        @pl.when(t == slot)
                        def _():
                            for part, i, j, half in ARRIVALS[slot]:
                                await_bytes(*chunk_piece(part, half, SLOT[i, j]))
                                for link, piece in onward(part, i, j, half):
                                    hand_on(part, i, j, link, piece)

        def stage(lag, work):
            @pl.when((t >= lag) & (t < CHUNKS + lag))
            def _():
                work(t - lag)

        stage(0, first_product)
        stage(LAG_SUM, chip_sum)
        stage(LAG_RELAY, relay_sum)
        stage(LAG_OWN, own_step)
        stage(LAG_PASS, pass_step)
        stage(LAG_FAR, pass_far)
        stage(LAG_UPDATE, second_product)
        return carry

    lax.fori_loop(0, CHUNKS + LAG_UPDATE, body, 0)

    stores = []
    for k in range(4):
        rows = pl.ds(256 * k, 256)
        update[:, rows] = total[:, rows].astype(BF16)
        stores.append(pltpu.make_async_copy(update.at[:, rows], update_hbm.at[:, rows], store_sem.at[2]))
        stores[-1].start()
    await_bytes(panel.at[pl.ds(1, CHUNKS - 1)], chunk_sent)
    await_bytes(pair_out, pair_sent)
    await_bytes(sum_out.at[pl.ds(0, CHUNKS - 4)], sum_sent)
    await_bytes(steps.at[pl.ds(0, CHUNKS - 4)], step_sent)
    await_bytes(first, store_sem.at[0])
    await_bytes(second, store_sem.at[1])
    await_bytes(update, store_sem.at[2])


def on_device(gradient, left_basis, first_moment, second_moment):
    dma = pltpu.SemaphoreType.DMA
    outs = pl.pallas_call(
        kernel,
        out_shape=(
            jax.ShapeDtypeStruct((COLS, ROWS), BF16),
            jax.ShapeDtypeStruct((COLS, ROWS), F32),
            jax.ShapeDtypeStruct((COLS, ROWS), F32),
        ),
        in_specs=[pl.BlockSpec(memory_space=pl.ANY)] * 4,
        out_specs=tuple([pl.BlockSpec(memory_space=pl.ANY)] * 3),
        scratch_shapes=[
            pltpu.VMEM((CHUNKS, ROWS, WIDE), BF16),
            pltpu.VMEM((COLS, ROWS), BF16),
            pltpu.VMEM((COLS, ROWS), BF16),
            pltpu.VMEM((COLS, ROWS), F32),
            pltpu.VMEM((COLS, ROWS), F32),
            pltpu.VMEM((2, HALF, WIDE), F32),
            pltpu.VMEM((CHUNKS, HALF, WIDE), BF16),
            pltpu.VMEM((CHUNKS, HALF, WIDE), BF16),
            pltpu.VMEM((CHUNKS, HALF, WIDE), BF16),
            pltpu.VMEM((CHUNKS, QUARTER, WIDE), BF16),
            pltpu.VMEM((4, 6, HALF, WIDE), BF16),
            pltpu.VMEM((CHUNKS, COLS, WIDE), BF16),
            pltpu.VMEM((COLS, ROWS), F32),
            pltpu.VMEM((COLS, ROWS), BF16),
            dma((4,)),
            dma((3,)),
            dma((CHUNKS, 4)),
            dma,
            dma((CHUNKS,)),
            dma,
            dma((CHUNKS,)),
            dma((4, 6, 2)),
            dma,
            dma((CHUNKS,)),
            dma((CHUNKS, 2)),
            dma((CHUNKS,)),
            dma,
        ],
        compiler_params=pltpu.CompilerParams(
            collective_id=0, has_side_effects=True, vmem_limit_bytes=60 << 20
        ),
        cost_estimate=pl.CostEstimate(flops=4 * 8192 * ROWS * COLS, bytes_accessed=10 << 20, transcendentals=0),
    )(gradient.T, left_basis, first_moment.T, second_moment.T)
    return tuple(out.T for out in outs)


def solution(mesh):
    placed = P("fsdp", ("tp", "layer"))
    return jax.shard_map(
        on_device, mesh=mesh, in_specs=(placed,) * 4, out_specs=(placed,) * 3, check_vma=False
    )
```
